32 devices in a mesh: section: 8 (over y, x, core), tensor: 4 (over z).
Axes of the slice: x: 2, y: 2, z: 4, core: 2. Of those that a mesh axis runs over, the one named last changes fastest.
Arguments:
- state: bfloat16 [8, 256, 6144], P('section', None, 'tensor'), may hold values from -6 to 6
- ln_gain: float32 [8, 6144], P('section'), may hold values from 0.1 to 1.9
- w_qkv: bfloat16 [8, 6144, 3, 4096], P('section', None, None, 'tensor'), may hold values from -0.078125 to 0.078125
- qk_gain: float32 [8, 2, 128], P('section'), may hold values from 0.5 to 1.5
- w_out: bfloat16 [8, 4096, 6144], P('section', 'tensor'), may hold values from -1 to 1
Outputs:
- advanced: bfloat16 [8, 256, 6144], P('section', None, 'tensor')
The draws below stay inside these ranges and needn't reach their ends.
All inputs are finite; a program needn't handle non-finite values.
Results may differ from the reference program's by a relative error of at most 0.03.
Values may be sent and summed in bfloat16 or wider, within the bound.
A program may use at most 192 MiB of HBM per device.

```python
import jax
import jax.numpy as jnp
from jax import lax

D = 6144
HEADS = 32
HD = 128
PATCHES = 256
STEPS = 2
SECTIONS = 8


def with_spikes(result, key, source, target, parts, factor):
    owner, partner = [(jnp.arange(result.shape[axis_at]) // (result.shape[axis_at] // parts)).reshape([-1 if axis == axis_at else 1 for axis in range(result.ndim)]) for axis_at in (source, target)]
    chosen = jax.random.permutation(key, parts)[partner]
    strong = (owner == chosen) | (owner == (partner + parts // 2) % parts)
    return jnp.where(strong, factor * result, result)


def level_of(key, dims, cuts, low, largest):
    factor_of = 1.0
    for position, shards_of in cuts:
        draws = jax.random.uniform(jax.random.fold_in(jax.random.fold_in(key, 6), position), (shards_of,), jnp.float32, low / len(cuts), largest / len(cuts))
        factor_of = factor_of * jnp.repeat(jnp.exp(draws), dims[position] // shards_of).reshape((-1,) + (1,) * (len(dims) - 1 - position))
    return factor_of


def gaussian(rng, dims, scale, reach, cuts=(), kind=jnp.bfloat16):
    drawn = jax.random.normal(rng, dims, jnp.float32) * scale
    if len(cuts) > 0:
        drawn = level_of(rng, dims, cuts, -0.22, 0.18) * drawn
    return jnp.clip(drawn, min=-reach, max=reach).astype(kind)


def gaussian_with(key, extent, scale, bound, split, heavy, dtype=jnp.bfloat16):
    array = scale * jax.random.normal(key, extent, jnp.float32)
    if split:
        array = array * level_of(key, extent, split, -0.22, 0.18)
    return jnp.clip(with_spikes(array, jax.random.fold_in(key, 3), *heavy), -bound, bound).astype(dtype)


def setup_inputs(seed: int = 0) -> dict:
    key_list = jax.random.split(jax.random.key(seed), 6)
    return {
        "state": gaussian(key_list[0], (SECTIONS, PATCHES, D), 1.0, 6.0, ((0, 8), (2, 4))),
        "ln_gain": jnp.clip(1.0 + 0.18 * jax.random.normal(key_list[1], (SECTIONS, D), jnp.float32), 0.1, 1.9),
        "w_qkv": gaussian(key_list[2], (SECTIONS, D, 3, HEADS * HD), D ** -0.5, 0.078125, ((0, 8), (3, 4))),
        "qk_gain": jnp.clip(1.0 + 0.1 * jax.random.normal(key_list[3], (SECTIONS, 2, HD), jnp.float32), 0.5, 1.5),
        "w_out": gaussian_with(key_list[4], (SECTIONS, HEADS * HD, D), (HEADS * HD // 64) ** -0.5, 1.0, ((0, 8), (1, 4)), (1, 2, 4, 2.0)),
    }


def layer_norm(values, gain):
    mean = lax.optimization_barrier(jnp.mean(values, axis=-1, keepdims=True))
    squares = lax.optimization_barrier(jnp.mean(values * values, axis=-1, keepdims=True))
    spread = squares - mean * mean
    return (values - mean) * lax.rsqrt(spread + 1e-06) * gain

def one_block(current, gain_row, qkv_weight, norm_gains, out_weight):
    patches = current.shape[0]
    normed = layer_norm(current.astype(jnp.float32), gain_row).astype(jnp.bfloat16)
    projected = jnp.dot(normed, qkv_weight.reshape(D, 3 * HEADS * HD), preferred_element_type=jnp.float32)
    projected = projected.reshape(patches, 3, HEADS, HD)
    query = layer_norm(projected[:, 0], norm_gains[0]).astype(jnp.bfloat16)
    keys_all = layer_norm(projected[:, 1], norm_gains[1]).astype(jnp.bfloat16)
    value = projected[:, 2].astype(jnp.bfloat16)
    scores = jnp.einsum('phe,qhe->hpq', query.astype(jnp.float32), keys_all.astype(jnp.float32)) / jnp.sqrt(jnp.float32(HD))
    expo = jnp.exp(scores)
    attend = (expo / lax.optimization_barrier(jnp.sum(expo, axis=-1, keepdims=True))).astype(jnp.bfloat16)
    mixed_rows = jnp.einsum('hpq,qhe->phe', attend.astype(jnp.float32), value.astype(jnp.float32))
    mixed_rows = mixed_rows.astype(jnp.bfloat16).reshape(patches, HEADS * HD)
    branch = jnp.dot(mixed_rows, out_weight, preferred_element_type=jnp.float32)
    return (current.astype(jnp.float32) + branch).astype(jnp.bfloat16)

def reference(state, ln_gain, w_qkv, qk_gain, w_out):
    current = state
    for step_index in range(STEPS):
        renewed = lax.map(lambda items: one_block(*items), (current, ln_gain, w_qkv, qk_gain, w_out))
        current = jnp.roll(renewed, 1, axis=0)
    return current
```

```python
import functools

import jax
import jax.numpy as jnp
from jax import lax
from jax.experimental import pallas as pl
from jax.experimental.pallas import tpu as pltpu
from jax.sharding import PartitionSpec as P

HD = 128
STEPS = 2
CHUNKS = 4
MESH = pl.DeviceIdType.MESH


def layer_norm(values, gain):
    mean = jnp.mean(values, axis=-1, keepdims=True)
    squares = jnp.mean(values * values, axis=-1, keepdims=True)
    spread = squares - mean * mean
    return (values - mean) * lax.rsqrt(spread + 1e-06) * gain


def relay_kernel(
    n, sections, chunks, gathers,
    mixed_ref, x_ref, w_ref, out_ref,
    slots, part, renewed,
    rs_send, rs_recv, ag_send, ag_recv, shift_send, shift_recv,
):
    t = lax.axis_index("tensor")
    s = lax.axis_index("section")
    patches, width = x_ref.shape
    rows = patches // chunks
    following, previous = lax.rem(s + 1, sections), lax.rem(s + sections - 1, sections)
    has_left, has_right = t > 0, t < n - 1

    def span(c):
        return pl.ds(c * rows, rows)

    def columns(f):
        return pl.ds(pl.multiple_of(f * width, 128), width)

    def rs_right(c, f):
        return pltpu.make_async_remote_copy(
            src_ref=slots.at[c, f + 1], dst_ref=slots.at[c, f + 1],
            send_sem=rs_send.at[c, f + 1], recv_sem=rs_recv.at[c, f + 1],
            device_id=(s, t + 1), device_id_type=MESH)

    def rs_left(c, f):
        return pltpu.make_async_remote_copy(
            src_ref=slots.at[c, f], dst_ref=slots.at[c, f],
            send_sem=rs_send.at[c, f], recv_sem=rs_recv.at[c, f],
            device_id=(s, t - 1), device_id_type=MESH)

    def ag_copy(c, f, step):
        block = out_ref.at[span(c), columns(f)]
        return pltpu.make_async_remote_copy(
            src_ref=block, dst_ref=block,
            send_sem=ag_send.at[c, f if step > 0 else f + 1], recv_sem=ag_recv.at[c, f],
            device_id=(s, t + step), device_id_type=MESH)

    def shift(c):
        target = out_ref.at[span(c), columns(t)] if gathers else out_ref.at[span(c), :]
        return pltpu.make_async_remote_copy(
            src_ref=renewed.at[span(c), :], dst_ref=target,
            send_sem=shift_send.at[c], recv_sem=shift_recv.at[c],
            device_id=(following, t), device_id_type=MESH)

    def products(c):
        def one(f, carry):
            part[c % 2, f] = jnp.dot(
                mixed_ref[span(c), :], w_ref[:, columns(f)], preferred_element_type=jnp.float32)
            return carry
        lax.fori_loop(0, n, one, 0)

    def end_sends(c):
        def one(i, carry):
            @pl.when(jnp.logical_not(has_left))
            def _():
                f = n - 1 - i
                slots[c, f + 1] = part[c % 2, f].astype(jnp.bfloat16)
                rs_right(c, f).start()

            @pl.when(jnp.logical_not(has_right))
            def _():
                slots[c, i] = part[c % 2, i].astype(jnp.bfloat16)
                rs_left(c, i).start()
            return carry
        lax.fori_loop(0, n - 1, one, 0)

    def forward_right(c, i):
        f = n - 1 - i

        @pl.when(jnp.logical_and(has_left, f > t))
        def _():
            rs_right(c, f).wait_recv()
            total = slots[c, f + 1].astype(jnp.float32) + part[c % 2, f]
            slots[c, f + 1] = total.astype(jnp.bfloat16)
            rs_right(c, f).start()

    def forward_left(c, i):
        @pl.when(jnp.logical_and(has_right, i < t))
        def _():
            rs_left(c, i).wait_recv()
            total = slots[c, i].astype(jnp.float32) + part[c % 2, i]
            slots[c, i] = total.astype(jnp.bfloat16)
            rs_left(c, i).start()

    def ag_start(c):
        shift(c).wait_recv()

        @pl.when(has_right)
        def _():
            ag_copy(c, t, 1).start()

        @pl.when(has_left)
        def _():
            ag_copy(c, t, -1).start()

    def ag_forward(c, d):
        @pl.when(t - d >= 0)
        def _():
            ag_copy(c, t - d, 1).wait_recv()

            @pl.when(has_right)
            def _():
                ag_copy(c, t - d, 1).start()

        @pl.when(t + d < n)
        def _():
            ag_copy(c, t + d, -1).wait_recv()

            @pl.when(has_left)
            def _():
                ag_copy(c, t + d, -1).start()

    def finish(c):
        total = x_ref[span(c), :].astype(jnp.float32) + part[c % 2, t]
        renewed[span(c), :] = total.astype(jnp.bfloat16)

        def take(slot):
            rs_left(c, slot).wait_recv()
            part[c % 2, t] = part[c % 2, t] + slots[c, slot].astype(jnp.float32)

        @pl.when(has_left)
        def _():
            take(t + 1)

        @pl.when(has_right)
        def _():
            take(t)
        total = x_ref[span(c), :].astype(jnp.float32) + part[c % 2, t]
        renewed[span(c), :] = total.astype(jnp.bfloat16)
        shift(c).start()

    barrier = pltpu.get_barrier_semaphore()
    for section in (following, previous):
        pl.semaphore_signal(barrier, inc=1, device_id=(section, t), device_id_type=MESH)

    @pl.when(has_left)
    def _():
        pl.semaphore_signal(barrier, inc=1, device_id=(s, t - 1), device_id_type=MESH)

    @pl.when(has_right)
    def _():
        pl.semaphore_signal(barrier, inc=1, device_id=(s, t + 1), device_id_type=MESH)
    products(0)
    pl.semaphore_wait(barrier, 2 + has_left.astype(jnp.int32) + has_right.astype(jnp.int32))

    for c in range(chunks + 1):
        if c < chunks:
            end_sends(c)
            if c + 1 < chunks:
                products(c + 1)
        if gathers and c > 0:
            ag_start(c - 1)

        def step(i, carry):
            if c < chunks:
                @pl.when(2 * t < n)
                def _():
                    forward_right(c, i)
                    forward_left(c, i)

                @pl.when(2 * t >= n)
                def _():
                    forward_left(c, i)
                    forward_right(c, i)
            if gathers and c > 0:
                ag_forward(c - 1, i + 1)
            return carry
        lax.fori_loop(0, n - 1, step, 0)
        if c < chunks:
            finish(c)

    def drain(c, carry):
        if not gathers:
            shift(c).wait_recv()
        shift(c).wait_send()

        def one(f, inner):
            @pl.when(f > t)
            def _():
                rs_right(c, f).wait_send()

            @pl.when(f < t)
            def _():
                rs_left(c, f).wait_send()
            if gathers:
                @pl.when(jnp.logical_and(has_right, f <= t))
                def _():
                    ag_copy(c, f, 1).wait_send()

                @pl.when(jnp.logical_and(has_left, f >= t))
                def _():
                    ag_copy(c, f, -1).wait_send()
            return inner
        return lax.fori_loop(0, n, one, carry)
    lax.fori_loop(0, chunks, drain, 0)


def relay(mixed, x, w_out, gathers):
    n, sections = lax.axis_size("tensor"), lax.axis_size("section")
    patches, width = x.shape
    rows = patches // CHUNKS
    dma = pltpu.SemaphoreType.DMA
    vmem = pl.BlockSpec(memory_space=pltpu.VMEM)
    return pl.pallas_call(
        functools.partial(relay_kernel, n, sections, CHUNKS, gathers),
        out_shape=jax.ShapeDtypeStruct((patches, n * width if gathers else width), jnp.bfloat16),
        in_specs=[vmem] * 3,
        out_specs=vmem,
        scratch_shapes=[
            pltpu.VMEM((CHUNKS, n + 1, rows, width), jnp.bfloat16),
            pltpu.VMEM((2, n, rows, width), jnp.float32),
            pltpu.VMEM((patches, width), jnp.bfloat16),
            dma((CHUNKS, n + 1)), dma((CHUNKS, n + 1)),
            dma((CHUNKS, n + 1)), dma((CHUNKS, n)),
            dma((CHUNKS,)), dma((CHUNKS,)),
        ],
        cost_estimate=pl.CostEstimate(
            flops=2 * patches * w_out.shape[0] * w_out.shape[1],
            bytes_accessed=2 * w_out.size, transcendentals=0),
        compiler_params=pltpu.CompilerParams(
            collective_id=1 if gathers else 0, has_side_effects=True,
            vmem_limit_bytes=48 * 1024 * 1024),
        name="relay_and_gather" if gathers else "relay",
    )(mixed, x, w_out)


def on_device(state, ln_gain, w_qkv, qk_gain, w_out):
    current = state[0]
    patches, width = current.shape
    full_width = w_qkv.shape[1]
    head_cols = w_qkv.shape[3]
    local_heads = head_cols // HD
    qkv_flat = w_qkv[0].reshape(full_width, 3 * head_cols)
    out_local = w_out[0]
    gain_row = ln_gain[0]
    norm_gains = qk_gain[0]
    gathered = lax.all_gather(current, "tensor", axis=1, tiled=True)
    for step_index in range(STEPS):
        normed = layer_norm(gathered.astype(jnp.float32), gain_row).astype(jnp.bfloat16)
        projected = jnp.dot(normed, qkv_flat, preferred_element_type=jnp.float32)
        projected = projected.reshape(patches, 3, local_heads, HD)
        query = layer_norm(projected[:, 0], norm_gains[0]).astype(jnp.bfloat16)
        keys_all = layer_norm(projected[:, 1], norm_gains[1]).astype(jnp.bfloat16)
        value = projected[:, 2].astype(jnp.bfloat16)
        scores = jnp.einsum(
            "phe,qhe->hpq", query, keys_all, preferred_element_type=jnp.float32
        ) / jnp.sqrt(jnp.float32(HD))
        expo = jnp.exp(scores)
        attend = (expo / jnp.sum(expo, axis=-1, keepdims=True)).astype(jnp.bfloat16)
        mixed_rows = jnp.einsum("hpq,qhe->phe", attend, value, preferred_element_type=jnp.float32)
        mixed_rows = mixed_rows.astype(jnp.bfloat16).reshape(patches, head_cols)
        last = step_index == STEPS - 1
        gathered = relay(mixed_rows, current, out_local, not last)
        if not last:
            start = lax.axis_index("tensor") * width
            current = lax.dynamic_slice_in_dim(gathered, start, width, axis=1)
    return gathered[None]


def solution(mesh):
    placed = (
        P("section", None, "tensor"),
        P("section", None),
        P("section", None, None, "tensor"),
        P("section", None, None),
        P("section", "tensor", None),
    )
    return jax.shard_map(
        on_device,
        mesh=mesh,
        in_specs=placed,
        out_specs=P("section", None, "tensor"),
        check_vma=False,
    )
```

```python
import functools

import jax
import jax.numpy as jnp
from jax import lax
from jax.experimental import pallas as pl
from jax.experimental.pallas import tpu as pltpu
from jax.sharding import PartitionSpec as P

HD = 128
STEPS = 2
CHUNKS = 4
MESH = pl.DeviceIdType.MESH


def layer_norm(values, gain):
    mean = jnp.mean(values, axis=-1, keepdims=True)
    squares = jnp.mean(values * values, axis=-1, keepdims=True)
    spread = squares - mean * mean
    return (values - mean) * lax.rsqrt(spread + 1e-06) * gain


def relay_kernel(
    n, sections, chunks, gathers,
    mixed_ref, x_ref, w_ref, out_ref,
    slots, part, renewed,
    rs_send, rs_recv, ag_send, ag_recv, shift_send, shift_recv,
):
    t = lax.axis_index("tensor")
    s = lax.axis_index("section")
    patches, width = x_ref.shape
    rows = patches // chunks
    following, previous = lax.rem(s + 1, sections), lax.rem(s + sections - 1, sections)
    has_left, has_right = t > 0, t < n - 1

    def span(c):
        return pl.ds(pl.multiple_of(c * rows, rows), rows)

    def columns(f):
        return pl.ds(pl.multiple_of(f * width, 128), width)

    def rs_right(c, f):
        return pltpu.make_async_remote_copy(
            src_ref=slots.at[c, f + 1], dst_ref=slots.at[c, f + 1],
            send_sem=rs_send.at[c, f + 1], recv_sem=rs_recv.at[c, f + 1],
            device_id=(s, t + 1), device_id_type=MESH)

    def rs_left(c, f):
        return pltpu.make_async_remote_copy(
            src_ref=slots.at[c, f], dst_ref=slots.at[c, f],
            send_sem=rs_send.at[c, f], recv_sem=rs_recv.at[c, f],
            device_id=(s, t - 1), device_id_type=MESH)

    def ag_copy(c, f, step):
        block = out_ref.at[span(c), columns(f)]
        return pltpu.make_async_remote_copy(
            src_ref=block, dst_ref=block,
            send_sem=ag_send.at[c, f if step > 0 else f + 1], recv_sem=ag_recv.at[c, f],
            device_id=(s, t + step), device_id_type=MESH)

    def shift(c):
        target = out_ref.at[span(c), columns(t)] if gathers else out_ref.at[span(c), :]
        return pltpu.make_async_remote_copy(
            src_ref=renewed.at[span(c), :], dst_ref=target,
            send_sem=shift_send.at[c], recv_sem=shift_recv.at[c],
            device_id=(following, t), device_id_type=MESH)

    def products(c):
        def one(f, carry):
            part[c % 3, f] = jnp.dot(
                mixed_ref[span(c), :], w_ref[:, columns(f)], preferred_element_type=jnp.float32)
            return carry
        lax.fori_loop(0, n, one, 0)

    def end_sends(c):
        def one(i, carry):
            @pl.when(jnp.logical_not(has_left))
            def _():
                f = n - 1 - i
                slots[c, f + 1] = part[c % 3, f].astype(jnp.bfloat16)
                rs_right(c, f).start()

            @pl.when(jnp.logical_not(has_right))
            def _():
                slots[c, i] = part[c % 3, i].astype(jnp.bfloat16)
                rs_left(c, i).start()
            return carry
        lax.fori_loop(0, n - 1, one, 0)

    def forward_right(c, i):
        f = n - 1 - i

        @pl.when(jnp.logical_and(has_left, f > t))
        def _():
            rs_right(c, f).wait_recv()
            total = slots[c, f + 1].astype(jnp.float32) + part[c % 3, f]
            slots[c, f + 1] = total.astype(jnp.bfloat16)
            rs_right(c, f).start()

    def forward_left(c, i):
        @pl.when(jnp.logical_and(has_right, i < t))
        def _():
            rs_left(c, i).wait_recv()
            total = slots[c, i].astype(jnp.float32) + part[c % 3, i]
            slots[c, i] = total.astype(jnp.bfloat16)
            rs_left(c, i).start()

    def ag_start(c):
        shift(c).wait_recv()

        @pl.when(has_right)
        def _():
            ag_copy(c, t, 1).start()

        @pl.when(has_left)
        def _():
            ag_copy(c, t, -1).start()

    def ag_forward(c, d):
        @pl.when(t - d >= 0)
        def _():
            ag_copy(c, t - d, 1).wait_recv()

            @pl.when(has_right)
            def _():
                ag_copy(c, t - d, 1).start()

        @pl.when(t + d < n)
        def _():
            ag_copy(c, t + d, -1).wait_recv()

            @pl.when(has_left)
            def _():
                ag_copy(c, t + d, -1).start()

    def finish(c):
        def take(slot):
            rs_left(c, slot).wait_recv()
            part[c % 3, t] = part[c % 3, t] + slots[c, slot].astype(jnp.float32)

        @pl.when(has_left)
        def _():
            take(t + 1)

        @pl.when(has_right)
        def _():
            take(t)
        total = x_ref[span(c), :].astype(jnp.float32) + part[c % 3, t]
        renewed[span(c), :] = total.astype(jnp.bfloat16)
        shift(c).start()

    barrier = pltpu.get_barrier_semaphore()
    for section in (following, previous):
        pl.semaphore_signal(barrier, inc=1, device_id=(section, t), device_id_type=MESH)

    @pl.when(has_left)
    def _():
        pl.semaphore_signal(barrier, inc=1, device_id=(s, t - 1), device_id_type=MESH)

    @pl.when(has_right)
    def _():
        pl.semaphore_signal(barrier, inc=1, device_id=(s, t + 1), device_id_type=MESH)
    products(0)
    pl.semaphore_wait(barrier, 2 + has_left.astype(jnp.int32) + has_right.astype(jnp.int32))

    end_sends(0)
    products(1)
    for c in range(chunks + n if gathers else chunks):
        if c + 1 < chunks:
            end_sends(c + 1)

        def step(i, carry):
            if gathers:
                older = c - 2 - i

                @pl.when(jnp.logical_and(older >= 0, older < chunks))
                def _():
                    ag_forward(older, i + 1)
            if c < chunks:
                @pl.when(2 * t < n)
                def _():
                    forward_right(c, i)
                    forward_left(c, i)

                @pl.when(2 * t >= n)
                def _():
                    forward_left(c, i)
                    forward_right(c, i)
            if gathers and 0 < c <= chunks:
                @pl.when(i == 0)
                def _():
                    ag_start(c - 1)
            return carry
        lax.fori_loop(0, n - 1, step, 0)
        if c + 2 < chunks:
            products(c + 2)
        if c < chunks:
            finish(c)

    def drain(c, carry):
        if not gathers:
            shift(c).wait_recv()
        shift(c).wait_send()

        def one(f, inner):
            @pl.when(f > t)
            def _():
                rs_right(c, f).wait_send()

            @pl.when(f < t)
            def _():
                rs_left(c, f).wait_send()
            if gathers:
                @pl.when(jnp.logical_and(has_right, f <= t))
                def _():
                    ag_copy(c, f, 1).wait_send()

                @pl.when(jnp.logical_and(has_left, f >= t))
                def _():
                    ag_copy(c, f, -1).wait_send()
            return inner
        return lax.fori_loop(0, n, one, carry)
    lax.fori_loop(0, chunks, drain, 0)


def relay(mixed, x, w_out, gathers):
    n, sections = lax.axis_size("tensor"), lax.axis_size("section")
    patches, width = x.shape
    rows = patches // CHUNKS
    dma = pltpu.SemaphoreType.DMA
    vmem = pl.BlockSpec(memory_space=pltpu.VMEM)
    return pl.pallas_call(
        functools.partial(relay_kernel, n, sections, CHUNKS, gathers),
        out_shape=jax.ShapeDtypeStruct((patches, n * width if gathers else width), jnp.bfloat16),
        in_specs=[vmem] * 3,
        out_specs=vmem,
        scratch_shapes=[
            pltpu.VMEM((CHUNKS, n + 1, rows, width), jnp.bfloat16),
            pltpu.VMEM((3, n, rows, width), jnp.float32),
            pltpu.VMEM((patches, width), jnp.bfloat16),
            dma((CHUNKS, n + 1)), dma((CHUNKS, n + 1)),
            dma((CHUNKS, n + 1)), dma((CHUNKS, n)),
            dma((CHUNKS,)), dma((CHUNKS,)),
        ],
        cost_estimate=pl.CostEstimate(
            flops=2 * patches * w_out.shape[0] * w_out.shape[1],
            bytes_accessed=2 * w_out.size, transcendentals=0),
        compiler_params=pltpu.CompilerParams(
            collective_id=1 if gathers else 0, has_side_effects=True,
            vmem_limit_bytes=48 * 1024 * 1024),
        name="relay_and_gather" if gathers else "relay",
    )(mixed, x, w_out)


def on_device(state, ln_gain, w_qkv, qk_gain, w_out):
    current = state[0]
    patches, width = current.shape
    full_width = w_qkv.shape[1]
    head_cols = w_qkv.shape[3]
    local_heads = head_cols // HD
    qkv_flat = w_qkv[0].reshape(full_width, 3 * head_cols)
    out_local = w_out[0]
    gain_row = ln_gain[0]
    norm_gains = qk_gain[0]
    gathered = lax.all_gather(current, "tensor", axis=1, tiled=True)
    for step_index in range(STEPS):
        normed = layer_norm(gathered.astype(jnp.float32), gain_row).astype(jnp.bfloat16)
        projected = jnp.dot(normed, qkv_flat, preferred_element_type=jnp.float32)
        projected = projected.reshape(patches, 3, local_heads, HD)
        query = layer_norm(projected[:, 0], norm_gains[0]).astype(jnp.bfloat16)
        keys_all = layer_norm(projected[:, 1], norm_gains[1]).astype(jnp.bfloat16)
        value = projected[:, 2].astype(jnp.bfloat16)
        scores = jnp.einsum(
            "phe,qhe->hpq", query, keys_all, preferred_element_type=jnp.float32
        ) / jnp.sqrt(jnp.float32(HD))
        expo = jnp.exp(scores)
        attend = (expo / jnp.sum(expo, axis=-1, keepdims=True)).astype(jnp.bfloat16)
        mixed_rows = jnp.einsum("hpq,qhe->phe", attend, value, preferred_element_type=jnp.float32)
        mixed_rows = mixed_rows.astype(jnp.bfloat16).reshape(patches, head_cols)
        last = step_index == STEPS - 1
        gathered = relay(mixed_rows, current, out_local, not last)
        if not last:
            start = lax.axis_index("tensor") * width
            current = lax.dynamic_slice_in_dim(gathered, start, width, axis=1)
    return gathered[None]


def solution(mesh):
    placed = (
        P("section", None, "tensor"),
        P("section", None),
        P("section", None, None, "tensor"),
        P("section", None, None),
        P("section", "tensor", None),
    )
    return jax.shard_map(
        on_device,
        mesh=mesh,
        in_specs=placed,
        out_specs=P("section", None, "tensor"),
        check_vma=False,
    )
```

```python
import functools

import jax
import jax.numpy as jnp
from jax import lax
from jax.experimental import pallas as pl
from jax.experimental.pallas import tpu as pltpu
from jax.sharding import PartitionSpec as P

HD = 128
STEPS = 2
CHUNKS = 8
MESH = pl.DeviceIdType.MESH


def layer_norm(values, gain):
    mean = jnp.mean(values, axis=-1, keepdims=True)
    squares = jnp.mean(values * values, axis=-1, keepdims=True)
    spread = squares - mean * mean
    return (values - mean) * lax.rsqrt(spread + 1e-06) * gain


def relay_kernel(
    n, sections, chunks, gathers,
    mixed_ref, x_ref, w_ref, out_ref,
    slots, part, renewed,
    rs_send, rs_recv, ag_send, ag_recv, shift_send, shift_recv,
):
    t = lax.axis_index("tensor")
    s = lax.axis_index("section")
    patches, width = x_ref.shape
    rows = patches // chunks
    following, previous = lax.rem(s + 1, sections), lax.rem(s + sections - 1, sections)
    has_left, has_right = t > 0, t < n - 1

    def span(c):
        return pl.ds(pl.multiple_of(c * rows, rows), rows)

    def columns(f):
        return pl.ds(pl.multiple_of(f * width, 128), width)

    def rs_right(c, f):
        return pltpu.make_async_remote_copy(
            src_ref=slots.at[c, f + 1], dst_ref=slots.at[c, f + 1],
            send_sem=rs_send.at[c, f + 1], recv_sem=rs_recv.at[c, f + 1],
            device_id=(s, t + 1), device_id_type=MESH)

    def rs_left(c, f):
        return pltpu.make_async_remote_copy(
            src_ref=slots.at[c, f], dst_ref=slots.at[c, f],
            send_sem=rs_send.at[c, f], recv_sem=rs_recv.at[c, f],
            device_id=(s, t - 1), device_id_type=MESH)

    def ag_copy(c, f, step):
        block = out_ref.at[span(c), columns(f)]
        return pltpu.make_async_remote_copy(
            src_ref=block, dst_ref=block,
            send_sem=ag_send.at[c, f if step > 0 else f + 1], recv_sem=ag_recv.at[c, f],
            device_id=(s, t + step), device_id_type=MESH)

    def shift(c):
        target = out_ref.at[span(c), columns(t)] if gathers else out_ref.at[span(c), :]
        return pltpu.make_async_remote_copy(
            src_ref=renewed.at[span(c), :], dst_ref=target,
            send_sem=shift_send.at[c], recv_sem=shift_recv.at[c],
            device_id=(following, t), device_id_type=MESH)

    def products(c):
        def one(f, carry):
            part[c % 3, f] = jnp.dot(
                mixed_ref[span(c), :], w_ref[:, columns(f)], preferred_element_type=jnp.float32)
            return carry
        lax.fori_loop(0, n, one, 0)

    def end_sends(c):
        def one(i, carry):
            @pl.when(jnp.logical_not(has_left))
            def _():
                f = n - 1 - i
                slots[c, f + 1] = part[c % 3, f].astype(jnp.bfloat16)
                rs_right(c, f).start()

            @pl.when(jnp.logical_not(has_right))
            def _():
                slots[c, i] = part[c % 3, i].astype(jnp.bfloat16)
                rs_left(c, i).start()
            return carry
        lax.fori_loop(0, n - 1, one, 0)

    def forward_right(c, i):
        f = n - 1 - i

        @pl.when(jnp.logical_and(has_left, f > t))
        def _():
            rs_right(c, f).wait_recv()
            total = slots[c, f + 1].astype(jnp.float32) + part[c % 3, f]
            slots[c, f + 1] = total.astype(jnp.bfloat16)
            rs_right(c, f).start()

    def forward_left(c, i):
        @pl.when(jnp.logical_and(has_right, i < t))
        def _():
            rs_left(c, i).wait_recv()
            total = slots[c, i].astype(jnp.float32) + part[c % 3, i]
            slots[c, i] = total.astype(jnp.bfloat16)
            rs_left(c, i).start()

    def ag_start(c):
        shift(c).wait_recv()

        @pl.when(has_right)
        def _():
            ag_copy(c, t, 1).start()

        @pl.when(has_left)
        def _():
            ag_copy(c, t, -1).start()

    def ag_forward(c, d):
        @pl.when(t - d >= 0)
        def _():
            ag_copy(c, t - d, 1).wait_recv()

            @pl.when(has_right)
            def _():
                ag_copy(c, t - d, 1).start()

        @pl.when(t + d < n)
        def _():
            ag_copy(c, t + d, -1).wait_recv()

            @pl.when(has_left)
            def _():
                ag_copy(c, t + d, -1).start()

    def finish(c):
        def take(slot):
            rs_left(c, slot).wait_recv()
            part[c % 3, t] = part[c % 3, t] + slots[c, slot].astype(jnp.float32)

        @pl.when(has_left)
        def _():
            take(t + 1)

        @pl.when(has_right)
        def _():
            take(t)
        total = x_ref[span(c), :].astype(jnp.float32) + part[c % 3, t]
        renewed[span(c), :] = total.astype(jnp.bfloat16)
        shift(c).start()

    barrier = pltpu.get_barrier_semaphore()
    for section in (following, previous):
        pl.semaphore_signal(barrier, inc=1, device_id=(section, t), device_id_type=MESH)

    @pl.when(has_left)
    def _():
        pl.semaphore_signal(barrier, inc=1, device_id=(s, t - 1), device_id_type=MESH)

    @pl.when(has_right)
    def _():
        pl.semaphore_signal(barrier, inc=1, device_id=(s, t + 1), device_id_type=MESH)
    products(0)
    pl.semaphore_wait(barrier, 2 + has_left.astype(jnp.int32) + has_right.astype(jnp.int32))

    end_sends(0)
    products(1)
    for c in range(chunks + n if gathers else chunks):
        if c + 1 < chunks:
            end_sends(c + 1)

        def step(i, carry):
            if gathers:
                older = c - 2 - i

                @pl.when(jnp.logical_and(older >= 0, older < chunks))
                def _():
                    ag_forward(older, i + 1)
            if c < chunks:
                @pl.when(2 * t < n)
                def _():
                    forward_right(c, i)
                    forward_left(c, i)

                @pl.when(2 * t >= n)
                def _():
                    forward_left(c, i)
                    forward_right(c, i)
            if gathers and 0 < c <= chunks:
                @pl.when(i == 0)
                def _():
                    ag_start(c - 1)
            return carry
        lax.fori_loop(0, n - 1, step, 0)
        if c + 2 < chunks:
            products(c + 2)
        if c < chunks:
            finish(c)

    def drain(c, carry):
        if not gathers:
            shift(c).wait_recv()
        shift(c).wait_send()

        def one(f, inner):
            @pl.when(f > t)
            def _():
                rs_right(c, f).wait_send()

            @pl.when(f < t)
            def _():
                rs_left(c, f).wait_send()
            if gathers:
                @pl.when(jnp.logical_and(has_right, f <= t))
                def _():
                    ag_copy(c, f, 1).wait_send()

                @pl.when(jnp.logical_and(has_left, f >= t))
                def _():
                    ag_copy(c, f, -1).wait_send()
            return inner
        return lax.fori_loop(0, n, one, carry)
    lax.fori_loop(0, chunks, drain, 0)


def relay(mixed, x, w_out, gathers):
    n, sections = lax.axis_size("tensor"), lax.axis_size("section")
    patches, width = x.shape
    rows = patches // CHUNKS
    dma = pltpu.SemaphoreType.DMA
    vmem = pl.BlockSpec(memory_space=pltpu.VMEM)
    return pl.pallas_call(
        functools.partial(relay_kernel, n, sections, CHUNKS, gathers),
        out_shape=jax.ShapeDtypeStruct((patches, n * width if gathers else width), jnp.bfloat16),
        in_specs=[vmem] * 3,
        out_specs=vmem,
        scratch_shapes=[
            pltpu.VMEM((CHUNKS, n + 1, rows, width), jnp.bfloat16),
            pltpu.VMEM((3, n, rows, width), jnp.float32),
            pltpu.VMEM((patches, width), jnp.bfloat16),
            dma((CHUNKS, n + 1)), dma((CHUNKS, n + 1)),
            dma((CHUNKS, n + 1)), dma((CHUNKS, n)),
            dma((CHUNKS,)), dma((CHUNKS,)),
        ],
        cost_estimate=pl.CostEstimate(
            flops=2 * patches * w_out.shape[0] * w_out.shape[1],
            bytes_accessed=2 * w_out.size, transcendentals=0),
        compiler_params=pltpu.CompilerParams(
            collective_id=1 if gathers else 0, has_side_effects=True,
            vmem_limit_bytes=48 * 1024 * 1024),
        name="relay_and_gather" if gathers else "relay",
    )(mixed, x, w_out)


def on_device(state, ln_gain, w_qkv, qk_gain, w_out):
    current = state[0]
    patches, width = current.shape
    full_width = w_qkv.shape[1]
    head_cols = w_qkv.shape[3]
    local_heads = head_cols // HD
    qkv_flat = w_qkv[0].reshape(full_width, 3 * head_cols)
    out_local = w_out[0]
    gain_row = ln_gain[0]
    norm_gains = qk_gain[0]
    gathered = lax.all_gather(current, "tensor", axis=1, tiled=True)
    for step_index in range(STEPS):
        normed = layer_norm(gathered.astype(jnp.float32), gain_row).astype(jnp.bfloat16)
        projected = jnp.dot(normed, qkv_flat, preferred_element_type=jnp.float32)
        projected = projected.reshape(patches, 3, local_heads, HD)
        query = layer_norm(projected[:, 0], norm_gains[0]).astype(jnp.bfloat16)
        keys_all = layer_norm(projected[:, 1], norm_gains[1]).astype(jnp.bfloat16)
        value = projected[:, 2].astype(jnp.bfloat16)
        scores = jnp.einsum(
            "phe,qhe->hpq", query, keys_all, preferred_element_type=jnp.float32
        ) / jnp.sqrt(jnp.float32(HD))
        expo = jnp.exp(scores)
        attend = (expo / jnp.sum(expo, axis=-1, keepdims=True)).astype(jnp.bfloat16)
        mixed_rows = jnp.einsum("hpq,qhe->phe", attend, value, preferred_element_type=jnp.float32)
        mixed_rows = mixed_rows.astype(jnp.bfloat16).reshape(patches, head_cols)
        last = step_index == STEPS - 1
        gathered = relay(mixed_rows, current, out_local, not last)
        if not last:
            start = lax.axis_index("tensor") * width
            current = lax.dynamic_slice_in_dim(gathered, start, width, axis=1)
    return gathered[None]


def solution(mesh):
    placed = (
        P("section", None, "tensor"),
        P("section", None),
        P("section", None, None, "tensor"),
        P("section", None, None),
        P("section", "tensor", None),
    )
    return jax.shard_map(
        on_device,
        mesh=mesh,
        in_specs=placed,
        out_specs=P("section", None, "tensor"),
        check_vma=False,
    )
```
